32 devices in a mesh: grp: 2 (over y), clip: 4 (over z), head: 4 (over x, core).
Axes of the slice: x: 2, y: 2, z: 4, core: 2. Of those that a mesh axis runs over, the one named last changes fastest.
Arguments:
- pair_clips: int32 [32], P('grp'), parts along dimension 0, may hold values from 0 to 3, as said below
- pair_rows: bfloat16 [32, 32, 8, 1280], P(('grp', 'clip'), None, 'head'), parts along dimension 0, may hold values from -5 to 5
- prefix_kv: bfloat16 [8, 1024, 8, 256], P(('grp', 'clip'), None, 'head'), parts along dimension 0, may hold values from -4 to 4
Outputs:
- attended: bfloat16 [32, 32, 8, 1024], P(('grp', 'clip'), None, 'head'), parts along dimension 0
The draws below stay inside these ranges and needn't reach their ends.
There are 2 independent parts, one for each index of `grp`. The reference program is written for one: setup_inputs(seed, part) draws one part's arguments, and reference() takes and returns one part's arrays. A program takes and returns all parts, laid end to end along the dimension named above; each array names one. Nothing has to cross between parts.
Inputs may be any that keep to these rules, and one draw needn't show every extreme that they name: `pair_clips`: within the 4 pairs of one device (aligned blocks), one clip, the same for every device and drawn from the seed, is named exactly twice, one other clip is not named, and every remaining clip is named exactly once.
All inputs are finite; a program needn't handle non-finite values.
Results may differ from the reference program's by a relative error of at most 0.0049.
Values may be sent and summed in bfloat16 or wider, within the bound.
A program may use at most 64 MiB of HBM per device.

```python
import jax
import jax.numpy as jnp
from jax import lax

KV_HEADS = 8
HEAD_DIM = 128
GROUP = 8
TB = 32
PREFIX = 1024
CLIPS = 4
PAIRS = 16


def draw_pair_clips(key, part):
    key = jax.random.fold_in(key, 3)
    key_hot = jax.random.fold_in(key, 11)
    key_skip = jax.random.fold_in(key, 12)
    key_order = jax.random.fold_in(key, 13)
    hot_clip = jax.random.randint(key_hot, (), 0, CLIPS)
    skipped = (hot_clip + 1 + jax.random.randint(key_skip, (CLIPS,), 0, CLIPS - 1)) % CLIPS
    owners = jnp.arange(CLIPS)
    owner_table = jnp.where(owners[None, :] == skipped[:, None], hot_clip, owners[None, :])
    row_keys = jax.random.split(key_order, CLIPS)
    owner_table = jax.vmap(lambda row_key, owner_row: jax.random.permutation(row_key, owner_row))(row_keys, owner_table)
    return owner_table.reshape(-1).astype(jnp.int32)


def draw_pair_rows(key, part):
    key = jax.random.fold_in(key, 5)
    full_shape = (PAIRS, TB, KV_HEADS, (GROUP + 2) * HEAD_DIM)
    values = jnp.clip(jax.random.normal(key, full_shape, jnp.float32), -4.0, 4.0)
    return values.astype(jnp.bfloat16)


def levels(own_key, dims, shards, smallest, largest):
    gain = 1.0
    for dim, shards_of in shards:
        steps = jax.random.uniform(jax.random.fold_in(jax.random.fold_in(own_key, 6), dim), (shards_of,), jnp.float32, smallest / len(shards), largest / len(shards))
        gain = gain * jnp.repeat(jnp.exp(steps), dims[dim] // shards_of).reshape((-1,) + (1,) * (len(dims) - 1 - dim))
    return gain


def normal_values(rng, shape, spread, most, shards=(), held_as=jnp.bfloat16):
    values = jax.random.normal(rng, shape, jnp.float32) * spread
    if len(shards) > 0:
        values = levels(rng, shape, shards, -0.22, 0.18) * values
    return jnp.clip(values, min=-most, max=most).astype(held_as)


def setup_inputs(seed: int = 0, part: int = 0) -> dict:
    splits = jax.random.split(jax.random.key(seed), 4)
    part_splits = jax.random.split(jax.random.fold_in(splits[3], part), 4)
    pair_clips = draw_pair_clips(jax.random.fold_in(jax.random.fold_in(splits[3], part), 71), part)
    pair_rows = draw_pair_rows(jax.random.fold_in(jax.random.fold_in(splits[3], part), 71), part)
    prefix_kv = normal_values(part_splits[2], (CLIPS, PREFIX, KV_HEADS, 2 * HEAD_DIM), 1.0, 4.0, ((0, 4), (2, 4)))
    return {"pair_clips": pair_clips, "pair_rows": pair_rows, "prefix_kv": prefix_kv}


def attend(queries, own_keys, own_values, pre_keys, pre_values):
    score_scale = queries.shape[-1] ** -0.5
    queries = queries.astype(jnp.float32)
    s_pre = jnp.einsum("btkgd,lkd->btkgl", queries, pre_keys.astype(jnp.float32)) * score_scale
    s_own = jnp.einsum("btkgd,bjkd->btkgj", queries, own_keys.astype(jnp.float32)) * score_scale
    tokens = queries.shape[1]
    causal = jnp.arange(tokens)[:, None] >= jnp.arange(tokens)[None, :]
    s_own = jnp.where(causal[None, :, None, None, :], s_own, -jnp.inf)
    row_max = jnp.maximum(jnp.max(s_pre, axis=-1), jnp.max(s_own, axis=-1))
    p_pre = jnp.exp(s_pre - row_max[..., None])
    p_own = jnp.exp(s_own - row_max[..., None])
    row_total = jnp.sum(p_pre, axis=-1) + jnp.sum(p_own, axis=-1)
    w_pre = (p_pre / row_total[..., None]).astype(jnp.bfloat16).astype(jnp.float32)
    w_own = (p_own / row_total[..., None]).astype(jnp.bfloat16).astype(jnp.float32)
    result = jnp.einsum("btkgl,lkd->btkgd", w_pre, pre_values.astype(jnp.float32))
    result = result + jnp.einsum("btkgj,bjkd->btkgd", w_own, own_values.astype(jnp.float32))
    return result.astype(jnp.bfloat16)


def reference(pair_clips, pair_rows, prefix_kv):
    def single_pair(packed):
        clip_id, pair_row = packed
        prefix = lax.dynamic_index_in_dim(prefix_kv, clip_id.astype(jnp.int32), 0, keepdims=False)
        queries = pair_row[:, :, :GROUP * HEAD_DIM].reshape(1, TB, KV_HEADS, GROUP, HEAD_DIM)
        own_keys = pair_row[None, :, :, GROUP * HEAD_DIM:(GROUP + 1) * HEAD_DIM]
        own_values = pair_row[None, :, :, (GROUP + 1) * HEAD_DIM:]
        output = attend(queries, own_keys, own_values, prefix[:, :, :HEAD_DIM], prefix[:, :, HEAD_DIM:])
        return output[0].reshape(TB, KV_HEADS, GROUP * HEAD_DIM)

    return lax.map(single_pair, (pair_clips, pair_rows))
```

```python
import functools
import math

import jax
import jax.numpy as jnp
from jax import lax
from jax.experimental import pallas as pl
from jax.experimental.pallas import tpu as pltpu
from jax.sharding import PartitionSpec as P

HEAD_DIM = 128
MESH = pl.DeviceIdType.MESH
NT = (((1,), (1,)), ((), ()))


def kernel(n, kv, group, clips_ref, rows_ref, pre_ref, out_ref,
           q_out, q_in, r_out, r_in, s_out, s_in, own_o, own_l, v_ext,
           qs_sem, qr_sem, rs_sem, rr_sem, ss_sem, sr_sem):
    me = lax.axis_index("clip")
    pairs, tokens, _ = rows_ref.shape
    dim = HEAD_DIM
    width = group * dim
    row_w = width + 2 * dim
    prefix = pre_ref.shape[0]
    scale = math.log2(math.e) / math.sqrt(dim)
    tiles = tokens // 8

    def q_copy(peer, r, slot):
        return pltpu.make_async_remote_copy(
            src_ref=q_out.at[peer, r], dst_ref=q_in.at[slot, r],
            send_sem=qs_sem.at[peer, r], recv_sem=qr_sem.at[slot, r],
            device_id={"clip": peer}, device_id_type=MESH)

    def r_copy(peer, r, slot):
        return pltpu.make_async_remote_copy(
            src_ref=r_out.at[peer, r], dst_ref=r_in.at[slot, r],
            send_sem=rs_sem.at[peer, r], recv_sem=rr_sem.at[slot, r],
            device_id={"clip": peer}, device_id_type=MESH)

    def s_copy(peer, r, slot):
        return pltpu.make_async_remote_copy(
            src_ref=s_out.at[peer, r], dst_ref=s_in.at[slot, r],
            send_sem=ss_sem.at[peer, r], recv_sem=sr_sem.at[slot, r],
            device_id={"clip": peer}, device_id_type=MESH)

    barrier = pltpu.get_barrier_semaphore()

    def greet(t, c):
        pl.semaphore_signal(barrier, inc=1, device_id={"clip": lax.rem(me + t, n)}, device_id_type=MESH)
        return c

    lax.fori_loop(1, n, greet, 0)

    base = me * pairs
    clips = [clips_ref[base + j] for j in range(pairs)]

    def pick(clip):
        first = jnp.int32(0)
        last = jnp.int32(0)
        for j in range(pairs):
            last = jnp.where(clips[j] == clip, j, last)
            first = jnp.where(clips[pairs - 1 - j] == clip, pairs - 1 - j, first)
        return first, last

    def pack(dst, peer):
        for r, pair in enumerate(pick(peer)):
            for k in range(kv):
                dst[peer, r, :, k * width:(k + 1) * width] = rows_ref[pair, :, k * row_w:k * row_w + width]

    def pack_peer(t, c):
        pack(q_out, lax.rem(me + t, n))
        return c

    lax.fori_loop(1, n, pack_peer, 0)
    pl.semaphore_wait(barrier, n - 1)

    def send_peer(t, c):
        peer = lax.rem(me + t, n)
        for r in range(2):
            q_copy(peer, r, me).start()
        return c

    lax.fori_loop(1, n, send_peer, 0)
    pack(q_in, me)

    for k in range(kv):
        v_ext[k, :, :dim] = pre_ref[:, k * 2 * dim + dim:(k + 1) * 2 * dim]
        v_ext[k, :, dim:] = jnp.ones((prefix, dim), jnp.bfloat16)

    def queries(ref, *at, start):
        return jnp.concatenate(
            [ref[(*at, slice(None), slice(start + g * dim, start + (g + 1) * dim))] for g in range(group)], axis=0)

    rows_of = group * tokens
    token = lax.rem(lax.broadcasted_iota(jnp.int32, (rows_of, tokens), 0), tokens)
    causal = token >= lax.broadcasted_iota(jnp.int32, (rows_of, tokens), 1)

    def attend_own(j, c):
        for k in range(kv):
            q = queries(rows_ref, j, start=k * row_w)
            keys = rows_ref[j, :, k * row_w + width:k * row_w + width + dim]
            values = rows_ref[j, :, k * row_w + width + dim:(k + 1) * row_w]
            s = lax.dot_general(q, keys, NT, preferred_element_type=jnp.float32)
            s = jnp.where(causal, s, -jnp.inf)
            top = jnp.max(s, axis=1, keepdims=True)
            p = jnp.exp2((s - top) * scale)
            total = jnp.broadcast_to(jnp.sum(p, axis=1, keepdims=True), (rows_of, dim))
            o = jnp.dot(p.astype(jnp.bfloat16), values, preferred_element_type=jnp.float32)
            own_o[j, k] = o / total
            own_l[j, k] = jnp.log2(total) + top * scale
        return c

    lax.fori_loop(0, pairs, attend_own, 0)

    lane = lax.broadcasted_iota(jnp.int32, (8, 128), 1)

    def serve(t, c):
        src = lax.rem(me - t + n, n)
        for r in range(2):
            @pl.when(t > 0)
            def _():
                q_copy(src, r, src).wait_recv()

            stats = jnp.zeros((8, 128), jnp.float32)
            for k in range(kv):
                q = queries(q_in, src, r, start=k * width)
                keys = pre_ref[:, k * 2 * dim:k * 2 * dim + dim]
                s = lax.dot_general(q, keys, NT, preferred_element_type=jnp.float32)
                top = jnp.max(s, axis=1, keepdims=True)
                p = jnp.exp2((s - top) * scale).astype(jnp.bfloat16)
                o = jnp.dot(p, v_ext[k], preferred_element_type=jnp.float32)
                total = o[:, dim:]
                o = (o[:, :dim] / total).astype(jnp.bfloat16)
                level = jnp.log2(total) + top * scale
                for g in range(group):
                    r_out[src, r, :, (k * group + g) * dim:(k * group + g + 1) * dim] = o[g * tokens:(g + 1) * tokens]
                    for i in range(tiles):
                        at = g * tokens + i * 8
                        stats = jnp.where(lane == i * kv * group + k * group + g, level[at:at + 8], stats)
            s_out[src, r] = stats

            @pl.when(t > 0)
            def _():
                s_copy(src, r, me).start()
                r_copy(src, r, me).start()
        return c

    lax.fori_loop(0, n, serve, 0)
    r_in[me] = r_out[me]
    s_in[me] = s_out[me]

    def finish(t, c):
        peer = lax.rem(me + t, n)
        for r in range(2):
            q_copy(peer, r, me).wait_send()
            r_copy(peer, r, peer).wait()
            s_copy(peer, r, peer).wait()
        return c

    lax.fori_loop(1, n, finish, 0)

    for j in range(pairs):
        rank = jnp.int32(0)
        for i in range(j):
            rank = jnp.where(clips[i] == clips[j], 1, rank)
        stats = s_in[clips[j], rank]
        for k in range(kv):
            for g in range(group):
                cols = slice((k * group + g) * dim, (k * group + g + 1) * dim)
                got = r_in[clips[j], rank, :, cols].astype(jnp.float32)
                level = jnp.concatenate(
                    [jnp.broadcast_to(stats[:, c:c + 1], (8, dim))
                     for c in (i * kv * group + k * group + g for i in range(tiles))], axis=0)
                rows = slice(g * tokens, (g + 1) * tokens)
                w_pre = 1.0 / (1.0 + jnp.exp2(own_l[j, k, rows] - level))
                mine = own_o[j, k, rows]
                out_ref[j, :, cols] = (mine + w_pre * (got - mine)).astype(jnp.bfloat16)


def on_device(n, pair_clips, pair_rows, prefix_kv):
    pairs, tokens, kv, row_w = pair_rows.shape
    group = row_w // HEAD_DIM - 2
    width = group * HEAD_DIM
    prefix = prefix_kv.shape[1]
    slots = (n, 2, tokens, kv * width)
    stats = (n, 2, 8, 128)
    own = (pairs, kv, group * tokens, HEAD_DIM)
    flops = 4 * n * 2 * kv * group * tokens * prefix * HEAD_DIM
    out = pl.pallas_call(
        functools.partial(kernel, n, kv, group),
        out_shape=jax.ShapeDtypeStruct((pairs, tokens, kv * width), jnp.bfloat16),
        in_specs=[pl.BlockSpec(memory_space=pltpu.SMEM)] + [pl.BlockSpec(memory_space=pltpu.VMEM)] * 2,
        out_specs=pl.BlockSpec(memory_space=pltpu.VMEM),
        scratch_shapes=[pltpu.VMEM(slots, jnp.bfloat16)] * 4 + [pltpu.VMEM(stats, jnp.float32)] * 2
        + [pltpu.VMEM(own, jnp.float32)] * 2
        + [pltpu.VMEM((kv, prefix, 2 * HEAD_DIM), jnp.bfloat16)]
        + [pltpu.SemaphoreType.DMA((n, 2))] * 6,
        compiler_params=pltpu.CompilerParams(
            collective_id=0, has_side_effects=True, vmem_limit_bytes=48 * 1024 * 1024),
        cost_estimate=pl.CostEstimate(
            flops=flops, bytes_accessed=4 * 1024 * 1024, transcendentals=0),
    )(pair_clips, pair_rows.reshape(pairs, tokens, kv * row_w), prefix_kv.reshape(prefix, kv * 2 * HEAD_DIM))
    return out.reshape(pairs, tokens, kv, width)


def solution(mesh):
    return jax.shard_map(
        functools.partial(on_device, mesh.shape["clip"]),
        mesh=mesh,
        in_specs=(
            P("grp"),
            P(("grp", "clip"), None, "head", None),
            P(("grp", "clip"), None, "head", None),
        ),
        out_specs=P(("grp", "clip"), None, "head", None),
        check_vma=False,
    )
```

```python
import functools
import math

import jax
import jax.numpy as jnp
from jax import lax
from jax.experimental import pallas as pl
from jax.experimental.pallas import tpu as pltpu
from jax.sharding import PartitionSpec as P

HEAD_DIM = 128
STAT_ROWS = 16
MESH = pl.DeviceIdType.MESH
NT = (((1,), (1,)), ((), ()))


def kernel(n, kv, group, clips_ref, rows_ref, pre_ref, out_ref,
           extra, q_out, q_in, r_out, r_in, e_out, e_in, own_o, own_l, v_ext,
           xs_sem, xr_sem, qs_sem, qr_sem, rs_sem, rr_sem, es_sem, er_sem):
    me = lax.axis_index("clip")
    pairs, tokens, _ = rows_ref.shape
    dim = HEAD_DIM
    width = group * dim
    row_w = width + 2 * dim
    prefix = pre_ref.shape[0]
    scale = math.log2(math.e) / math.sqrt(dim)
    rows_of = group * tokens
    tiles = rows_of // 8
    assert 3 * tiles <= 128

    def x_copy(to, src, side, k):
        return pltpu.make_async_remote_copy(
            src_ref=extra.at[src, k], dst_ref=extra.at[src, k],
            send_sem=xs_sem.at[side, src, k], recv_sem=xr_sem.at[src, k],
            device_id={"clip": to}, device_id_type=MESH)

    def q_copy(peer, slot, k):
        return pltpu.make_async_remote_copy(
            src_ref=q_out.at[peer, k], dst_ref=q_in.at[slot, k],
            send_sem=qs_sem.at[peer, k], recv_sem=qr_sem.at[slot, k],
            device_id={"clip": peer}, device_id_type=MESH)

    def r_copy(peer, slot, k):
        return pltpu.make_async_remote_copy(
            src_ref=r_out.at[peer, k], dst_ref=r_in.at[slot, k],
            send_sem=rs_sem.at[peer, k], recv_sem=rr_sem.at[slot, k],
            device_id={"clip": peer}, device_id_type=MESH)

    def e_copy(to, dest, side, k):
        return pltpu.make_async_remote_copy(
            src_ref=e_out.at[dest, k], dst_ref=e_in.at[side, dest, k],
            send_sem=es_sem.at[dest, k], recv_sem=er_sem.at[side, dest, k],
            device_id={"clip": to}, device_id_type=MESH)

    def inside(i):
        return jnp.logical_and(i >= 0, i < n)

    barrier = pltpu.get_barrier_semaphore()

    def greet(t, c):
        pl.semaphore_signal(barrier, inc=1, device_id={"clip": lax.rem(me + t, n)}, device_id_type=MESH)
        return c

    lax.fori_loop(1, n, greet, 0)

    base = me * pairs
    clips = [clips_ref[base + j] for j in range(pairs)]
    ranks = []
    hot = jnp.int32(0)
    extra_pair = jnp.int32(0)
    for j in range(pairs):
        again = jnp.int32(0)
        for i in range(j):
            again = jnp.where(clips[i] == clips[j], 1, again)
        ranks.append(again)
        hot = jnp.where(again == 1, clips[j], hot)
        extra_pair = jnp.where(again == 1, j, extra_pair)

    def pack(dst, slot, pair):
        for k in range(kv):
            for g in range(group):
                at = k * row_w + g * dim
                dst[slot, k, g * tokens:(g + 1) * tokens] = rows_ref[pair, :, at:at + dim]

    def pack_first(dst, peer):
        first = jnp.int32(0)
        for j in reversed(range(pairs)):
            first = jnp.where(clips[j] == peer, j, first)
        pack(dst, peer, first)

    def pack_peer(t, c):
        pack_first(q_out, lax.rem(me + t, n))
        return c

    pack(extra, me, extra_pair)
    lax.fori_loop(1, n, pack_peer, 0)
    pl.semaphore_wait(barrier, n - 1)

    def send_extra(side, c):
        to = me + 2 * side - 1

        @pl.when(inside(to))
        def _():
            for k in range(kv):
                x_copy(to, me, side, k).start()
        return c

    def send_first(t, c):
        peer = lax.rem(me + t, n)
        for k in range(kv):
            q_copy(peer, me, k).start()
        return c

    lax.fori_loop(0, 2, send_extra, 0)
    lax.fori_loop(1, n, send_first, 0)
    pack_first(q_in, me)

    for k in range(kv):
        v_ext[k, :, :dim] = pre_ref[:, k * 2 * dim + dim:(k + 1) * 2 * dim]
        v_ext[k, :, dim:] = jnp.ones((prefix, dim), jnp.bfloat16)

    token = lax.rem(lax.broadcasted_iota(jnp.int32, (rows_of, tokens), 0), tokens)
    causal = token >= lax.broadcasted_iota(jnp.int32, (rows_of, tokens), 1)
    lane = lax.broadcasted_iota(jnp.int32, (8, 128), 1)
    lane_tile = lax.rem(lane, tiles)

    def attend_own(j, c):
        for k in range(kv):
            q = jnp.concatenate(
                [rows_ref[j, :, k * row_w + g * dim:k * row_w + (g + 1) * dim] for g in range(group)], axis=0)
            keys = rows_ref[j, :, k * row_w + width:k * row_w + width + dim]
            values = rows_ref[j, :, k * row_w + width + dim:(k + 1) * row_w]
            s = lax.dot_general(q, keys, NT, preferred_element_type=jnp.float32)
            s = jnp.where(causal, s, -jnp.inf)
            top = jnp.max(s, axis=1, keepdims=True)
            p = jnp.exp2((s - top) * scale)
            total = jnp.broadcast_to(jnp.sum(p, axis=1, keepdims=True), (rows_of, dim))
            o = jnp.dot(p.astype(jnp.bfloat16), values, preferred_element_type=jnp.float32)
            own_o[j, k] = o / total
            own_l[j, k] = jnp.log2(total) + top * scale
        return c

    def attend(src_ref, src, dst_ref, k):
        keys = pre_ref[:, k * 2 * dim:k * 2 * dim + dim]
        s = lax.dot_general(src_ref[src, k], keys, NT, preferred_element_type=jnp.float32)
        top = jnp.max(s, axis=1, keepdims=True)
        p = jnp.exp2((s - top) * scale).astype(jnp.bfloat16)
        o = jnp.dot(p, v_ext[k], preferred_element_type=jnp.float32)
        total = o[:, dim:]
        dst_ref[src, k, :rows_of] = (o[:, :dim] / total).astype(jnp.bfloat16)
        level = jnp.log2(total) + top * scale
        stats = jnp.zeros((8, 128), jnp.float32)
        for i in range(tiles):
            stats = jnp.where(lane_tile == i, level[i * 8:(i + 1) * 8], stats)
        high = stats.astype(jnp.bfloat16).astype(jnp.float32)
        middle = (stats - high).astype(jnp.bfloat16).astype(jnp.float32)
        low = stats - high - middle
        parts = jnp.where(lane < tiles, high, jnp.where(lane < 2 * tiles, middle, low))
        dst_ref[src, k, rows_of:] = jnp.concatenate([parts, jnp.zeros_like(parts)], axis=0).astype(jnp.bfloat16)

    def serve_extra(t):
        def one(side, c):
            step = 2 * side - 1
            peer = me + step * t

            @pl.when(inside(peer))
            def _():
                for k in range(kv):
                    x_copy(peer, peer, 1 - side, k).wait_recv()

                    @pl.when(inside(me - step))
                    def _():
                        x_copy(me - step, peer, 1 - side, k).start()

                for k in range(kv):
                    attend(extra, peer, e_out, k)

                    @pl.when(jnp.logical_not(inside(me - step)))
                    def _():
                        e_copy(me + step, peer, side, k).start()
            return c

        lax.fori_loop(0, 2, one, 0)

    def serve_first(t):
        def one(side, c):
            peer = me + (2 * side - 1) * t

            @pl.when(inside(peer))
            def _():
                for k in range(kv):
                    q_copy(peer, peer, k).wait_recv()
                    attend(q_in, peer, r_out, k)
                    r_copy(peer, me, k).start()
            return c

        lax.fori_loop(0, 2, one, 0)

    lax.fori_loop(0, pairs, attend_own, 0)
    for k in range(kv):
        attend(extra, me, e_out, k)
        attend(q_in, me, r_out, k)

    def serve(t, c):
        serve_extra(t)
        serve_first(t)
        return c

    lax.fori_loop(1, n, serve, 0)
    r_in[me] = r_out[me]

    def relay(i, c):
        t = n - 1 - i

        def one(side, d):
            step = 2 * side - 1
            peer = me + step * t

            @pl.when(jnp.logical_and(inside(peer), inside(me - step)))
            def _():
                for k in range(kv):
                    e_copy(me - step, peer, side, k).wait_recv()
                    e_out[peer, k] = jnp.where(hot == me, e_out[peer, k], e_in[side, peer, k])
                    e_copy(me + step, peer, side, k).start()
            return d

        return lax.fori_loop(0, 2, one, c)

    lax.fori_loop(0, n - 1, relay, 0)
    r_in[n] = e_out[me]

    def collect(side, c):
        step = 2 * side - 1

        @pl.when(inside(me - step))
        def _():
            for k in range(kv):
                e_copy(me - step, me, side, k).wait_recv()
                r_in[n, k] = jnp.where((me - hot) * step > 0, e_in[side, me, k], r_in[n, k])
        return c

    lax.fori_loop(0, 2, collect, 0)

    def finish(t, c):
        peer = lax.rem(me + t, n)
        for k in range(kv):
            r_copy(peer, peer, k).wait()
            q_copy(peer, me, k).wait_send()
            e_copy(peer, peer, 0, k).wait_send()
        return c

    lax.fori_loop(1, n, finish, 0)

    def finish_extra(src, c):
        def one(side, d):
            step = 2 * side - 1

            @pl.when(jnp.logical_and((me - src) * step >= 0, inside(me + step)))
            def _():
                for k in range(kv):
                    x_copy(me + step, src, side, k).wait_send()
            return d

        return lax.fori_loop(0, 2, one, c)

    lax.fori_loop(0, n, finish_extra, 0)

    for j in range(pairs):
        slot = jnp.where(ranks[j] == 1, n, clips[j])
        for k in range(kv):
            parts = r_in[slot, k, rows_of:].astype(jnp.float32)[:8]
            stats = parts + pltpu.roll(parts, 128 - tiles, 1) + pltpu.roll(parts, 128 - 2 * tiles, 1)
            for g in range(group):
                rows = slice(g * tokens, (g + 1) * tokens)
                level = jnp.concatenate(
                    [jnp.broadcast_to(stats[:, c:c + 1], (8, dim))
                     for c in range(g * tokens // 8, (g + 1) * tokens // 8)], axis=0)
                w_pre = 1.0 / (1.0 + jnp.exp2(own_l[j, k, rows] - level))
                mine = own_o[j, k, rows]
                got = r_in[slot, k, rows].astype(jnp.float32)
                cols = slice((k * group + g) * dim, (k * group + g + 1) * dim)
                out_ref[j, :, cols] = (mine + w_pre * (got - mine)).astype(jnp.bfloat16)


def on_device(n, pair_clips, pair_rows, prefix_kv):
    pairs, tokens, kv, row_w = pair_rows.shape
    group = row_w // HEAD_DIM - 2
    width = group * HEAD_DIM
    prefix = prefix_kv.shape[1]
    rows_of = group * tokens
    queries = pltpu.VMEM((n, kv, rows_of, HEAD_DIM), jnp.bfloat16)
    result = (kv, rows_of + STAT_ROWS, HEAD_DIM)
    own = pltpu.VMEM((pairs, kv, rows_of, HEAD_DIM), jnp.float32)
    sems = pltpu.SemaphoreType.DMA((n, kv))
    sems_two = pltpu.SemaphoreType.DMA((2, n, kv))
    flops = 4 * n * 2 * kv * rows_of * prefix * HEAD_DIM
    out = pl.pallas_call(
        functools.partial(kernel, n, kv, group),
        out_shape=jax.ShapeDtypeStruct((pairs, tokens, kv * width), jnp.bfloat16),
        in_specs=[pl.BlockSpec(memory_space=pltpu.SMEM)] + [pl.BlockSpec(memory_space=pltpu.VMEM)] * 2,
        out_specs=pl.BlockSpec(memory_space=pltpu.VMEM),
        scratch_shapes=[
            queries, queries, queries,
            pltpu.VMEM((n,) + result, jnp.bfloat16),
            pltpu.VMEM((n + 1,) + result, jnp.bfloat16),
            pltpu.VMEM((n,) + result, jnp.bfloat16),
            pltpu.VMEM((2, n) + result, jnp.bfloat16),
            own, own,
            pltpu.VMEM((kv, prefix, 2 * HEAD_DIM), jnp.bfloat16),
            sems_two, sems, sems, sems, sems, sems, sems, sems_two,
        ],
        compiler_params=pltpu.CompilerParams(
            collective_id=0, has_side_effects=True, vmem_limit_bytes=48 * 1024 * 1024),
        cost_estimate=pl.CostEstimate(
            flops=flops, bytes_accessed=4 * 1024 * 1024, transcendentals=0),
    )(pair_clips, pair_rows.reshape(pairs, tokens, kv * row_w), prefix_kv.reshape(prefix, kv * 2 * HEAD_DIM))
    return out.reshape(pairs, tokens, kv, width)


def solution(mesh):
    return jax.shard_map(
        functools.partial(on_device, mesh.shape["clip"]),
        mesh=mesh,
        in_specs=(
            P("grp"),
            P(("grp", "clip"), None, "head", None),
            P(("grp", "clip"), None, "head", None),
        ),
        out_specs=P(("grp", "clip"), None, "head", None),
        check_vma=False,
    )
```

```python
import functools
import math

import jax
import jax.numpy as jnp
from jax import lax
from jax.experimental import pallas as pl
from jax.experimental.pallas import tpu as pltpu
from jax.sharding import PartitionSpec as P

HEAD_DIM = 128
STAT_ROWS = 16
MESH = pl.DeviceIdType.MESH
NT = (((1,), (1,)), ((), ()))


def kernel(n, kv, group, clips_ref, rows_ref, pre_ref, out_ref,
           extra, q_out, q_in, first, ab_out, ab_in, own_o, own_l, v_ext,
           qs_sem, qr_sem, as_sem, ar_sem):
    me = lax.axis_index("clip")
    pairs, tokens, _ = rows_ref.shape
    dim = HEAD_DIM
    width = group * dim
    row_w = width + 2 * dim
    prefix = pre_ref.shape[0]
    scale = math.log2(math.e) / math.sqrt(dim)
    rows_of = group * tokens
    tiles = rows_of // 8
    assert 3 * tiles <= 128

    def q_copy(peer, slot, k):
        return pltpu.make_async_remote_copy(
            src_ref=q_out.at[peer, k], dst_ref=q_in.at[slot, k],
            send_sem=qs_sem.at[peer, k], recv_sem=qr_sem.at[slot, k],
            device_id={"clip": peer}, device_id_type=MESH)

    def ab_copy(which, peer, slot, k):
        return pltpu.make_async_remote_copy(
            src_ref=ab_out.at[which, peer, k], dst_ref=ab_in.at[which, slot, k],
            send_sem=as_sem.at[which, peer, k], recv_sem=ar_sem.at[which, slot, k],
            device_id={"clip": peer}, device_id_type=MESH)

    def inside(i):
        return jnp.logical_and(i >= 0, i < n)

    barrier = pltpu.get_barrier_semaphore()

    def greet(t, c):
        pl.semaphore_signal(barrier, inc=1, device_id={"clip": lax.rem(me + t, n)}, device_id_type=MESH)
        return c

    lax.fori_loop(1, n, greet, 0)

    base = me * pairs
    clips = [clips_ref[base + j] for j in range(pairs)]
    ranks = []
    hot = jnp.int32(0)
    extra_pair = jnp.int32(0)
    for j in range(pairs):
        again = jnp.int32(0)
        for i in range(j):
            again = jnp.where(clips[i] == clips[j], 1, again)
        ranks.append(again)
        hot = jnp.where(again == 1, clips[j], hot)
        extra_pair = jnp.where(again == 1, j, extra_pair)

    def pack(dst, slot, pair):
        for k in range(kv):
            for g in range(group):
                at = k * row_w + g * dim
                dst[slot, k, g * tokens:(g + 1) * tokens] = rows_ref[pair, :, at:at + dim]

    def pack_first(dst, peer):
        first = jnp.int32(0)
        for j in reversed(range(pairs)):
            first = jnp.where(clips[j] == peer, j, first)
        pack(dst, peer, first)

    def pack_peer(t, c):
        pack_first(q_out, lax.rem(me + t, n))
        return c

    lax.fori_loop(1, n, pack_peer, 0)
    pl.semaphore_wait(barrier, n - 1)

    def peers(body):
        def at(t, c):
            def one(side, d):
                peer = me + (2 * side - 1) * t

                @pl.when(inside(peer))
                def _():
                    body(peer)
                return d

            return lax.fori_loop(0, 2, one, c)

        lax.fori_loop(1, n, at, 0)

    for k in range(kv):
        peers(lambda peer, k=k: q_copy(peer, me, k).start())
    pack_first(q_in, me)
    pack(extra, 0, extra_pair)

    for k in range(kv):
        v_ext[k, :, :dim] = pre_ref[:, k * 2 * dim + dim:(k + 1) * 2 * dim]
        v_ext[k, :, dim:] = jnp.ones((prefix, dim), jnp.bfloat16)

    token = lax.rem(lax.broadcasted_iota(jnp.int32, (rows_of, tokens), 0), tokens)
    causal = token >= lax.broadcasted_iota(jnp.int32, (rows_of, tokens), 1)
    lane = lax.broadcasted_iota(jnp.int32, (8, 128), 1)
    lane_tile = lax.rem(lane, tiles)

    def attend_own(j, c):
        for k in range(kv):
            q = jnp.concatenate(
                [rows_ref[j, :, k * row_w + g * dim:k * row_w + (g + 1) * dim] for g in range(group)], axis=0)
            keys = rows_ref[j, :, k * row_w + width:k * row_w + width + dim]
            values = rows_ref[j, :, k * row_w + width + dim:(k + 1) * row_w]
            s = lax.dot_general(q, keys, NT, preferred_element_type=jnp.float32)
            s = jnp.where(causal, s, -jnp.inf)
            top = jnp.max(s, axis=1, keepdims=True)
            p = jnp.exp2((s - top) * scale)
            total = jnp.broadcast_to(jnp.sum(p, axis=1, keepdims=True), (rows_of, dim))
            o = jnp.dot(p.astype(jnp.bfloat16), values, preferred_element_type=jnp.float32)
            own_o[j, k] = o / total
            own_l[j, k] = jnp.log2(total) + top * scale
        return c

    def attend(q, k, put):
        keys = pre_ref[:, k * 2 * dim:k * 2 * dim + dim]
        s = lax.dot_general(q, keys, NT, preferred_element_type=jnp.float32)
        top = jnp.max(s, axis=1, keepdims=True)
        p = jnp.exp2((s - top) * scale).astype(jnp.bfloat16)
        o = jnp.dot(p, v_ext[k], preferred_element_type=jnp.float32)
        total = o[:, dim:]
        put(slice(0, rows_of), (o[:, :dim] / total).astype(jnp.bfloat16))
        level = jnp.log2(total) + top * scale
        stats = jnp.zeros((8, 128), jnp.float32)
        for i in range(tiles):
            stats = jnp.where(lane_tile == i, level[i * 8:(i + 1) * 8], stats)
        high = stats.astype(jnp.bfloat16).astype(jnp.float32)
        middle = (stats - high).astype(jnp.bfloat16).astype(jnp.float32)
        low = stats - high - middle
        parts = jnp.where(lane < tiles, high, jnp.where(lane < 2 * tiles, middle, low))
        put(slice(rows_of, rows_of + STAT_ROWS),
            jnp.concatenate([parts, jnp.zeros_like(parts)], axis=0).astype(jnp.bfloat16))

    lax.fori_loop(0, pairs, attend_own, 0)
    for k in range(kv):
        def put_first(rows, value, k=k):
            ab_in[0, me, k, rows] = value
            ab_in[1, me, k, rows] = value

        def put_extra(rows, value, k=k):
            ab_in[1, n, k, rows] = value

        attend(q_in[me, k], k, put_first)
        attend(extra[0, k], k, put_extra)

    def serve_first(peer, k):
        q_copy(peer, peer, k).wait_recv()

        def put(rows, value):
            first[peer, k, rows] = value
            if rows.start == 0:
                value = jnp.where(hot == peer, extra[0, k], value)
            ab_out[0, peer, k, rows] = value

        attend(q_in[peer, k], k, put)
        ab_copy(0, peer, me, k).start()

    def serve_extra(peer, k):
        ab_copy(0, peer, peer, k).wait_recv()

        def put(rows, value):
            ab_out[1, peer, k, rows] = jnp.where(hot == peer, first[peer, k, rows], value)

        attend(ab_in[0, peer, k, :rows_of], k, put)
        ab_copy(1, peer, me, k).start()

    for k in range(kv):
        peers(functools.partial(serve_first, k=k))
    for k in range(kv):
        peers(functools.partial(serve_extra, k=k))

    def finish(peer):
        for k in range(kv):
            q_copy(peer, me, k).wait_send()
            ab_copy(0, peer, me, k).wait_send()
            ab_copy(1, peer, peer, k).wait()

    peers(finish)

    for j in range(pairs):
        which = jnp.where(hot == me, 1, ranks[j])
        slot = jnp.where(jnp.logical_and(hot == me, ranks[j] == 1), n, clips[j])
        for k in range(kv):
            parts = ab_in[which, slot, k, rows_of:].astype(jnp.float32)[:8]
            stats = parts + pltpu.roll(parts, 128 - tiles, 1) + pltpu.roll(parts, 128 - 2 * tiles, 1)
            for g in range(group):
                rows = slice(g * tokens, (g + 1) * tokens)
                level = jnp.concatenate(
                    [jnp.broadcast_to(stats[:, c:c + 1], (8, dim))
                     for c in range(g * tokens // 8, (g + 1) * tokens // 8)], axis=0)
                w_pre = 1.0 / (1.0 + jnp.exp2(own_l[j, k, rows] - level))
                mine = own_o[j, k, rows]
                got = ab_in[which, slot, k, rows].astype(jnp.float32)
                cols = slice((k * group + g) * dim, (k * group + g + 1) * dim)
                out_ref[j, :, cols] = (mine + w_pre * (got - mine)).astype(jnp.bfloat16)


def on_device(n, pair_clips, pair_rows, prefix_kv):
    pairs, tokens, kv, row_w = pair_rows.shape
    group = row_w // HEAD_DIM - 2
    width = group * HEAD_DIM
    prefix = prefix_kv.shape[1]
    rows_of = group * tokens
    queries = pltpu.VMEM((n, kv, rows_of, HEAD_DIM), jnp.bfloat16)
    result = (kv, rows_of + STAT_ROWS, HEAD_DIM)
    own = pltpu.VMEM((pairs, kv, rows_of, HEAD_DIM), jnp.float32)
    sems = pltpu.SemaphoreType.DMA((n, kv))
    sems_two = pltpu.SemaphoreType.DMA((2, n, kv))
    flops = 4 * n * 2 * kv * rows_of * prefix * HEAD_DIM
    out = pl.pallas_call(
        functools.partial(kernel, n, kv, group),
        out_shape=jax.ShapeDtypeStruct((pairs, tokens, kv * width), jnp.bfloat16),
        in_specs=[pl.BlockSpec(memory_space=pltpu.SMEM)] + [pl.BlockSpec(memory_space=pltpu.VMEM)] * 2,
        out_specs=pl.BlockSpec(memory_space=pltpu.VMEM),
        scratch_shapes=[
            pltpu.VMEM((1, kv, rows_of, HEAD_DIM), jnp.bfloat16),
            queries, queries,
            pltpu.VMEM((n,) + result, jnp.bfloat16),
            pltpu.VMEM((2, n) + result, jnp.bfloat16),
            pltpu.VMEM((2, n + 1) + result, jnp.bfloat16),
            own, own,
            pltpu.VMEM((kv, prefix, 2 * HEAD_DIM), jnp.bfloat16),
            sems, sems, sems_two, sems_two,
        ],
        compiler_params=pltpu.CompilerParams(
            collective_id=0, has_side_effects=True, vmem_limit_bytes=48 * 1024 * 1024),
        cost_estimate=pl.CostEstimate(
            flops=flops, bytes_accessed=4 * 1024 * 1024, transcendentals=0),
    )(pair_clips, pair_rows.reshape(pairs, tokens, kv * row_w), prefix_kv.reshape(prefix, kv * 2 * HEAD_DIM))
    return out.reshape(pairs, tokens, kv, width)


def solution(mesh):
    return jax.shard_map(
        functools.partial(on_device, mesh.shape["clip"]),
        mesh=mesh,
        in_specs=(
            P("grp"),
            P(("grp", "clip"), None, "head", None),
            P(("grp", "clip"), None, "head", None),
        ),
        out_specs=P(("grp", "clip"), None, "head", None),
        check_vma=False,
    )
```

```python
import functools
import math

import jax
import jax.numpy as jnp
from jax import lax
from jax.experimental import pallas as pl
from jax.experimental.pallas import tpu as pltpu
from jax.sharding import PartitionSpec as P

HEAD_DIM = 128
STAT_ROWS = 16
MESH = pl.DeviceIdType.MESH
NT = (((1,), (1,)), ((), ()))


def kernel(n, kv, group, clips_ref, rows_ref, pre_ref, out_ref,
           extra, q_out, q_in, first, ab_out, ab_in, own_o, own_l, v_ext, sums,
           qs_sem, qr_sem, as_sem, ar_sem):
    me = lax.axis_index("clip")
    pairs, tokens = rows_ref.shape[:2]
    dim = HEAD_DIM
    width = group * dim
    row_w = width + 2 * dim
    prefix = pre_ref.shape[0]
    scale = math.log2(math.e) / math.sqrt(dim)
    rows_of = group * tokens
    tiles = rows_of // 8
    assert 3 * tiles <= 128 and kv * 8 <= STAT_ROWS

    def q_copy(peer, slot, k):
        return pltpu.make_async_remote_copy(
            src_ref=q_out.at[peer, k], dst_ref=q_in.at[slot, k],
            send_sem=qs_sem.at[peer, k], recv_sem=qr_sem.at[slot, k],
            device_id={"clip": peer}, device_id_type=MESH)

    def rows_sent(k):
        return rows_of + (STAT_ROWS if k == kv - 1 else 0)

    def ab_copy(which, peer, slot, k):
        return pltpu.make_async_remote_copy(
            src_ref=ab_out.at[which, peer, k, pl.ds(0, rows_sent(k))],
            dst_ref=ab_in.at[which, slot, k, pl.ds(0, rows_sent(k))],
            send_sem=as_sem.at[which, peer, k], recv_sem=ar_sem.at[which, slot, k],
            device_id={"clip": peer}, device_id_type=MESH)

    def inside(i):
        return jnp.logical_and(i >= 0, i < n)

    barrier = pltpu.get_barrier_semaphore()

    def greet(t, c):
        pl.semaphore_signal(barrier, inc=1, device_id={"clip": lax.rem(me + t, n)}, device_id_type=MESH)
        return c

    lax.fori_loop(1, n, greet, 0)

    base = me * pairs
    clips = [clips_ref[base + j] for j in range(pairs)]
    ranks = []
    hot = jnp.int32(0)
    extra_pair = jnp.int32(0)
    for j in range(pairs):
        again = jnp.int32(0)
        for i in range(j):
            again = jnp.where(clips[i] == clips[j], 1, again)
        ranks.append(again)
        hot = jnp.where(again == 1, clips[j], hot)
        extra_pair = jnp.where(again == 1, j, extra_pair)

    def pack(dst, slot, pair, k):
        for g in range(group):
            dst[slot, k, g * tokens:(g + 1) * tokens] = rows_ref[pair, :, k, g * dim:(g + 1) * dim]

    def pack_first(dst, peer, k):
        pair = jnp.int32(0)
        for j in reversed(range(pairs)):
            pair = jnp.where(clips[j] == peer, j, pair)
        pack(dst, peer, pair, k)

    def peers(body):
        def at(t, c):
            def one(side, d):
                peer = me + (2 * side - 1) * t

                @pl.when(inside(peer))
                def _():
                    body(peer)
                return d

            return lax.fori_loop(0, 2, one, c)

        lax.fori_loop(1, n, at, 0)

    for k in range(kv):
        peers(functools.partial(pack_first, q_out, k=k))
        if k == 0:
            pl.semaphore_wait(barrier, n - 1)
        peers(lambda peer, k=k: q_copy(peer, me, k).start())
    for k in range(kv):
        pack_first(q_in, me, k)
        pack(extra, 0, extra_pair, k)

    for k in range(kv):
        v_ext[k, :, :dim] = pre_ref[:, k * 2 * dim + dim:(k + 1) * 2 * dim]
        v_ext[k, :, dim:] = jnp.ones((prefix, dim), jnp.bfloat16)

    token = lax.rem(lax.broadcasted_iota(jnp.int32, (rows_of, tokens), 0), tokens)
    causal = token >= lax.broadcasted_iota(jnp.int32, (rows_of, tokens), 1)
    lane = lax.broadcasted_iota(jnp.int32, (8, 128), 1)
    lane_tile = lax.rem(lane, tiles)

    def attend_own(j, c):
        for k in range(kv):
            q = jnp.concatenate(
                [rows_ref[j, :, k, g * dim:(g + 1) * dim] for g in range(group)], axis=0)
            keys = rows_ref[j, :, k, width:width + dim]
            values = rows_ref[j, :, k, width + dim:]
            s = lax.dot_general(q, keys, NT, preferred_element_type=jnp.float32)
            s = jnp.where(causal, s, -jnp.inf)
            top = jnp.max(s, axis=1, keepdims=True)
            p = jnp.exp2((s - top) * scale)
            total = jnp.broadcast_to(jnp.sum(p, axis=1, keepdims=True), (rows_of, dim))
            o = jnp.dot(p.astype(jnp.bfloat16), values, preferred_element_type=jnp.float32)
            own_o[j, k] = o / total
            own_l[j, k] = jnp.log2(total) + top * scale
        return c

    def attend(q, k, at, put):
        keys = pre_ref[:, k * 2 * dim:k * 2 * dim + dim]
        s = lax.dot_general(q, keys, NT, preferred_element_type=jnp.float32)
        top = jnp.max(s, axis=1, keepdims=True)
        p = jnp.exp2((s - top) * scale).astype(jnp.bfloat16)
        o = jnp.dot(p, v_ext[k], preferred_element_type=jnp.float32)
        total = o[:, dim:]
        put(slice(0, rows_of), (o[:, :dim] / total).astype(jnp.bfloat16))
        level = jnp.log2(total) + top * scale
        stats = jnp.zeros((8, 128), jnp.float32)
        for i in range(tiles):
            stats = jnp.where(lane_tile == i, level[i * 8:(i + 1) * 8], stats)
        high = stats.astype(jnp.bfloat16).astype(jnp.float32)
        middle = (stats - high).astype(jnp.bfloat16).astype(jnp.float32)
        low = stats - high - middle
        parts = jnp.where(lane < tiles, high, jnp.where(lane < 2 * tiles, middle, low))
        if k < kv - 1:
            sums[(*at, k)] = parts
        else:
            block = [sums[(*at, i)] for i in range(k)] + [parts]
            block += [jnp.zeros_like(parts)] * (STAT_ROWS // 8 - kv)
            put(slice(rows_of, rows_of + STAT_ROWS), jnp.concatenate(block, axis=0).astype(jnp.bfloat16))

    lax.fori_loop(0, pairs, attend_own, 0)
    for k in range(kv):
        def put_first(rows, value, k=k):
            ab_in[0, me, k, rows] = value
            ab_in[1, me, k, rows] = value

        def put_extra(rows, value, k=k):
            ab_in[1, n, k, rows] = value

        attend(q_in[me, k], k, (0, me), put_first)
        attend(extra[0, k], k, (1, me), put_extra)

    def serve_first(peer, k):
        q_copy(peer, peer, k).wait_recv()

        def put(rows, value):
            first[peer, k, rows] = value
            if rows.start == 0:
                value = jnp.where(hot == peer, extra[0, k], value)
            ab_out[0, peer, k, rows] = value

        attend(q_in[peer, k], k, (0, peer), put)
        ab_copy(0, peer, me, k).start()

    def serve_extra(peer, k):
        ab_copy(0, peer, peer, k).wait_recv()

        def put(rows, value):
            ab_out[1, peer, k, rows] = jnp.where(hot == peer, first[peer, k, rows], value)

        attend(ab_in[0, peer, k, :rows_of], k, (1, peer), put)
        ab_copy(1, peer, me, k).start()

    for k in range(kv):
        peers(functools.partial(serve_first, k=k))
    for k in range(kv):
        peers(functools.partial(serve_extra, k=k))

    def finish(peer):
        for k in range(kv):
            q_copy(peer, me, k).wait_send()
            ab_copy(0, peer, me, k).wait_send()
            ab_copy(1, peer, peer, k).wait()

    peers(finish)

    for j in range(pairs):
        which = jnp.where(hot == me, 1, ranks[j])
        slot = jnp.where(jnp.logical_and(hot == me, ranks[j] == 1), n, clips[j])
        for k in range(kv):
            parts = ab_in[which, slot, kv - 1, rows_of:].astype(jnp.float32)[k * 8:(k + 1) * 8]
            stats = parts + pltpu.roll(parts, 128 - tiles, 1) + pltpu.roll(parts, 128 - 2 * tiles, 1)
            for g in range(group):
                rows = slice(g * tokens, (g + 1) * tokens)
                level = jnp.concatenate(
                    [jnp.broadcast_to(stats[:, c:c + 1], (8, dim))
                     for c in range(g * tokens // 8, (g + 1) * tokens // 8)], axis=0)
                w_pre = 1.0 / (1.0 + jnp.exp2(own_l[j, k, rows] - level))
                mine = own_o[j, k, rows]
                got = ab_in[which, slot, k, rows].astype(jnp.float32)
                cols = slice((k * group + g) * dim, (k * group + g + 1) * dim)
                out_ref[j, :, cols] = (mine + w_pre * (got - mine)).astype(jnp.bfloat16)


def on_device(n, pair_clips, pair_rows, prefix_kv):
    pairs, tokens, kv, row_w = pair_rows.shape
    group = row_w // HEAD_DIM - 2
    width = group * HEAD_DIM
    prefix = prefix_kv.shape[1]
    rows_of = group * tokens
    queries = pltpu.VMEM((n, kv, rows_of, HEAD_DIM), jnp.bfloat16)
    result = (kv, rows_of + STAT_ROWS, HEAD_DIM)
    own = pltpu.VMEM((pairs, kv, rows_of, HEAD_DIM), jnp.float32)
    sems = pltpu.SemaphoreType.DMA((n, kv))
    sems_two = pltpu.SemaphoreType.DMA((2, n, kv))
    flops = 4 * n * 2 * kv * rows_of * prefix * HEAD_DIM
    out = pl.pallas_call(
        functools.partial(kernel, n, kv, group),
        out_shape=jax.ShapeDtypeStruct((pairs, tokens, kv * width), jnp.bfloat16),
        in_specs=[pl.BlockSpec(memory_space=pltpu.SMEM)] + [pl.BlockSpec(memory_space=pltpu.VMEM)] * 2,
        out_specs=pl.BlockSpec(memory_space=pltpu.VMEM),
        scratch_shapes=[
            pltpu.VMEM((1, kv, rows_of, HEAD_DIM), jnp.bfloat16),
            queries, queries,
            pltpu.VMEM((n,) + result, jnp.bfloat16),
            pltpu.VMEM((2, n) + result, jnp.bfloat16),
            pltpu.VMEM((2, n + 1) + result, jnp.bfloat16),
            own, own,
            pltpu.VMEM((kv, prefix, 2 * HEAD_DIM), jnp.bfloat16),
            pltpu.VMEM((2, n, kv, 8, 128), jnp.float32),
            sems, sems, sems_two, sems_two,
        ],
        compiler_params=pltpu.CompilerParams(
            collective_id=0, has_side_effects=True, vmem_limit_bytes=48 * 1024 * 1024),
        cost_estimate=pl.CostEstimate(
            flops=flops, bytes_accessed=4 * 1024 * 1024, transcendentals=0),
    )(pair_clips, pair_rows, prefix_kv.reshape(prefix, kv * 2 * HEAD_DIM))
    return out.reshape(pairs, tokens, kv, width)


def solution(mesh):
    return jax.shard_map(
        functools.partial(on_device, mesh.shape["clip"]),
        mesh=mesh,
        in_specs=(
            P("grp"),
            P(("grp", "clip"), None, "head", None),
            P(("grp", "clip"), None, "head", None),
        ),
        out_specs=P(("grp", "clip"), None, "head", None),
        check_vma=False,
    )
```

```python
import functools
import math

import jax
import jax.numpy as jnp
from jax import lax
from jax.experimental import pallas as pl
from jax.experimental.pallas import tpu as pltpu
from jax.sharding import PartitionSpec as P

HEAD_DIM = 128
STAT_ROWS = 16
MESH = pl.DeviceIdType.MESH
NT = (((1,), (1,)), ((), ()))


def kernel(n, kv, group, clips_ref, rows_ref, pre_ref, out_ref,
           extra, q_out, q_in, first, ab_out, ab_in, own_o, own_l, v_ext, sums,
           qs_sem, qr_sem, as_sem, ar_sem):
    me = lax.axis_index("clip")
    pairs, tokens = rows_ref.shape[:2]
    dim = HEAD_DIM
    width = group * dim
    row_w = width + 2 * dim
    prefix = pre_ref.shape[0]
    scale = math.log2(math.e) / math.sqrt(dim)
    rows_of = group * tokens
    tiles = rows_of // 8
    assert 3 * tiles <= 128 and kv * 8 <= STAT_ROWS

    def q_copy(peer, slot, k):
        return pltpu.make_async_remote_copy(
            src_ref=q_out.at[peer, k], dst_ref=q_in.at[slot, k],
            send_sem=qs_sem.at[peer, k], recv_sem=qr_sem.at[slot, k],
            device_id={"clip": peer}, device_id_type=MESH)

    def rows_sent(k):
        return rows_of + (STAT_ROWS if k == kv - 1 else 0)

    def ab_copy(which, peer, slot, k):
        return pltpu.make_async_remote_copy(
            src_ref=ab_out.at[which, peer, k, pl.ds(0, rows_sent(k))],
            dst_ref=ab_in.at[which, slot, k, pl.ds(0, rows_sent(k))],
            send_sem=as_sem.at[which, peer, k], recv_sem=ar_sem.at[which, slot, k],
            device_id={"clip": peer}, device_id_type=MESH)

    def inside(i):
        return jnp.logical_and(i >= 0, i < n)

    barrier = pltpu.get_barrier_semaphore()

    def greet(t, c):
        pl.semaphore_signal(barrier, inc=1, device_id={"clip": lax.rem(me + t, n)}, device_id_type=MESH)
        return c

    lax.fori_loop(1, n, greet, 0)

    base = me * pairs
    clips = [clips_ref[base + j] for j in range(pairs)]
    ranks = []
    hot = jnp.int32(0)
    extra_pair = jnp.int32(0)
    for j in range(pairs):
        again = jnp.int32(0)
        for i in range(j):
            again = jnp.where(clips[i] == clips[j], 1, again)
        ranks.append(again)
        hot = jnp.where(again == 1, clips[j], hot)
        extra_pair = jnp.where(again == 1, j, extra_pair)

    def pack(dst, slot, pair, k):
        for g in range(group):
            dst[slot, k, g * tokens:(g + 1) * tokens] = rows_ref[pair, :, k, g * dim:(g + 1) * dim]

    def pack_first(dst, peer, k):
        pair = jnp.int32(0)
        for j in reversed(range(pairs)):
            pair = jnp.where(clips[j] == peer, j, pair)
        pack(dst, peer, pair, k)

    def peers(body):
        def at(t, c):
            def one(side, d):
                peer = me + (2 * side - 1) * t

                @pl.when(inside(peer))
                def _():
                    body(peer)
                return d

            return lax.fori_loop(0, 2, one, c)

        lax.fori_loop(1, n, at, 0)

    for k in range(kv):
        peers(functools.partial(pack_first, q_out, k=k))
        if k == 0:
            pl.semaphore_wait(barrier, n - 1)
        peers(lambda peer, k=k: q_copy(peer, me, k).start())
    for k in range(kv):
        pack_first(q_in, me, k)
        pack(extra, 0, extra_pair, k)

    for k in range(kv):
        v_ext[k, :, :dim] = pre_ref[:, k * 2 * dim + dim:(k + 1) * 2 * dim]
        v_ext[k, :, dim:] = jnp.ones((prefix, dim), jnp.bfloat16)

    token = lax.rem(lax.broadcasted_iota(jnp.int32, (rows_of, tokens), 0), tokens)
    causal = token >= lax.broadcasted_iota(jnp.int32, (rows_of, tokens), 1)
    lane = lax.broadcasted_iota(jnp.int32, (8, 128), 1)
    lane_tile = lax.rem(lane, tiles)

    def attend_own(j, c):
        for k in range(kv):
            q = jnp.concatenate(
                [rows_ref[j, :, k, g * dim:(g + 1) * dim] for g in range(group)], axis=0)
            keys = rows_ref[j, :, k, width:width + dim]
            values = rows_ref[j, :, k, width + dim:]
            s = lax.dot_general(q, keys, NT, preferred_element_type=jnp.float32)
            s = jnp.where(causal, s, -jnp.inf)
            top = jnp.max(s, axis=1, keepdims=True)
            p = jnp.exp2((s - top) * scale)
            total = jnp.broadcast_to(jnp.sum(p, axis=1, keepdims=True), (rows_of, dim))
            o = jnp.dot(p.astype(jnp.bfloat16), values, preferred_element_type=jnp.float32)
            own_o[j, k] = o / total
            own_l[j, k] = jnp.log2(total) + top * scale
        return c

    def attend(q, k, at, put):
        keys = pre_ref[:, k * 2 * dim:k * 2 * dim + dim]
        s = lax.dot_general(q, keys, NT, preferred_element_type=jnp.float32)
        top = jnp.max(s, axis=1, keepdims=True)
        p = jnp.exp2((s - top) * scale).astype(jnp.bfloat16)
        o = jnp.dot(p, v_ext[k], preferred_element_type=jnp.float32)
        total = o[:, dim:]
        put(slice(0, rows_of), (o[:, :dim] / total).astype(jnp.bfloat16))
        level = jnp.log2(total) + top * scale
        stats = jnp.zeros((8, 128), jnp.float32)
        for i in range(tiles):
            stats = jnp.where(lane_tile == i, level[i * 8:(i + 1) * 8], stats)
        high = stats.astype(jnp.bfloat16).astype(jnp.float32)
        middle = (stats - high).astype(jnp.bfloat16).astype(jnp.float32)
        low = stats - high - middle
        parts = jnp.where(lane < tiles, high, jnp.where(lane < 2 * tiles, middle, low))
        if k < kv - 1:
            sums[(*at, k)] = parts
        else:
            block = [sums[(*at, i)] for i in range(k)] + [parts]
            block += [jnp.zeros_like(parts)] * (STAT_ROWS // 8 - kv)
            put(slice(rows_of, rows_of + STAT_ROWS), jnp.concatenate(block, axis=0).astype(jnp.bfloat16))

    lax.fori_loop(0, pairs, attend_own, 0)
    for k in range(kv):
        def put_first(rows, value, k=k):
            ab_in[0, me, k, rows] = value
            ab_in[1, me, k, rows] = value

        def put_extra(rows, value, k=k):
            ab_in[1, n, k, rows] = value

        attend(q_in[me, k], k, (0, me), put_first)
        attend(extra[0, k], k, (1, me), put_extra)

    def serve_first(peer, k):
        q_copy(peer, peer, k).wait_recv()

        def put(rows, value):
            first[peer, k, rows] = value
            if rows.start == 0:
                value = jnp.where(hot == peer, extra[0, k], value)
            ab_out[0, peer, k, rows] = value

        attend(q_in[peer, k], k, (0, peer), put)
        ab_copy(0, peer, me, k).start()

    def serve_extra(peer, k):
        ab_copy(0, peer, peer, k).wait_recv()

        def put(rows, value):
            ab_out[1, peer, k, rows] = jnp.where(hot == peer, first[peer, k, rows], value)

        attend(ab_in[0, peer, k, :rows_of], k, (1, peer), put)
        ab_copy(1, peer, me, k).start()

    peers(lambda peer: [serve_first(peer, k) for k in range(kv)])
    peers(lambda peer: [serve_extra(peer, k) for k in range(kv)])

    def finish(peer):
        for k in range(kv):
            q_copy(peer, me, k).wait_send()
            ab_copy(0, peer, me, k).wait_send()
            ab_copy(1, peer, peer, k).wait()

    peers(finish)

    for j in range(pairs):
        which = jnp.where(hot == me, 1, ranks[j])
        slot = jnp.where(jnp.logical_and(hot == me, ranks[j] == 1), n, clips[j])
        for k in range(kv):
            parts = ab_in[which, slot, kv - 1, rows_of:].astype(jnp.float32)[k * 8:(k + 1) * 8]
            stats = parts + pltpu.roll(parts, 128 - tiles, 1) + pltpu.roll(parts, 128 - 2 * tiles, 1)
            for g in range(group):
                rows = slice(g * tokens, (g + 1) * tokens)
                level = jnp.concatenate(
                    [jnp.broadcast_to(stats[:, c:c + 1], (8, dim))
                     for c in range(g * tokens // 8, (g + 1) * tokens // 8)], axis=0)
                w_pre = 1.0 / (1.0 + jnp.exp2(own_l[j, k, rows] - level))
                mine = own_o[j, k, rows]
                got = ab_in[which, slot, k, rows].astype(jnp.float32)
                cols = slice((k * group + g) * dim, (k * group + g + 1) * dim)
                out_ref[j, :, cols] = (mine + w_pre * (got - mine)).astype(jnp.bfloat16)


def on_device(n, pair_clips, pair_rows, prefix_kv):
    pairs, tokens, kv, row_w = pair_rows.shape
    group = row_w // HEAD_DIM - 2
    width = group * HEAD_DIM
    prefix = prefix_kv.shape[1]
    rows_of = group * tokens
    queries = pltpu.VMEM((n, kv, rows_of, HEAD_DIM), jnp.bfloat16)
    result = (kv, rows_of + STAT_ROWS, HEAD_DIM)
    own = pltpu.VMEM((pairs, kv, rows_of, HEAD_DIM), jnp.float32)
    sems = pltpu.SemaphoreType.DMA((n, kv))
    sems_two = pltpu.SemaphoreType.DMA((2, n, kv))
    flops = 4 * n * 2 * kv * rows_of * prefix * HEAD_DIM
    out = pl.pallas_call(
        functools.partial(kernel, n, kv, group),
        out_shape=jax.ShapeDtypeStruct((pairs, tokens, kv * width), jnp.bfloat16),
        in_specs=[pl.BlockSpec(memory_space=pltpu.SMEM)] + [pl.BlockSpec(memory_space=pltpu.VMEM)] * 2,
        out_specs=pl.BlockSpec(memory_space=pltpu.VMEM),
        scratch_shapes=[
            pltpu.VMEM((1, kv, rows_of, HEAD_DIM), jnp.bfloat16),
            queries, queries,
            pltpu.VMEM((n,) + result, jnp.bfloat16),
            pltpu.VMEM((2, n) + result, jnp.bfloat16),
            pltpu.VMEM((2, n + 1) + result, jnp.bfloat16),
            own, own,
            pltpu.VMEM((kv, prefix, 2 * HEAD_DIM), jnp.bfloat16),
            pltpu.VMEM((2, n, kv, 8, 128), jnp.float32),
            sems, sems, sems_two, sems_two,
        ],
        compiler_params=pltpu.CompilerParams(
            collective_id=0, has_side_effects=True, vmem_limit_bytes=48 * 1024 * 1024),
        cost_estimate=pl.CostEstimate(
            flops=flops, bytes_accessed=4 * 1024 * 1024, transcendentals=0),
    )(pair_clips, pair_rows, prefix_kv.reshape(prefix, kv * 2 * HEAD_DIM))
    return out.reshape(pairs, tokens, kv, width)


def solution(mesh):
    return jax.shard_map(
        functools.partial(on_device, mesh.shape["clip"]),
        mesh=mesh,
        in_specs=(
            P("grp"),
            P(("grp", "clip"), None, "head", None),
            P(("grp", "clip"), None, "head", None),
        ),
        out_specs=P(("grp", "clip"), None, "head", None),
        check_vma=False,
    )
```
